256 devices in a mesh: pipe: 16 (over y, z_lo), expert: 16 (over x, z_hi, core).
Axes of the slice: x: 4, y: 4, z: 8 (z_hi: 2, z_lo: 4; z = z_hi * 4 + z_lo), core: 2. Of those that a mesh axis runs over, the one named last changes fastest.
Arguments:
- tokens: bfloat16 [16, 2048, 2048], P('pipe', 'expert'), may hold values from -6 to 6
- grad_out: bfloat16 [16, 2048, 2048], P('pipe', 'expert'), may hold values from -6 to 6
- route_ids: int32 [16, 2048, 2], P('pipe', 'expert'), may hold values from 0 to 15, all different within a row; in each aligned block of 128 rows (0 to 127, 128 to 255, ..., all dimensions but the last counted through in order) at most 32 rows name the same one
- route_probs: float32 [16, 2048, 2], P('pipe', 'expert'), may hold values from 0.1 to 1
- w_gate: bfloat16 [16, 16, 1024, 768], P('pipe', 'expert'), may hold values from -0.125 to 0.125
- w_up: bfloat16 [16, 16, 1024, 768], P('pipe', 'expert'), may hold values from -0.125 to 0.125
- w_down: bfloat16 [16, 16, 768, 1024], P('pipe', 'expert'), may hold values from -0.21875 to 0.21875
Outputs:
- grad_tokens: bfloat16 [16, 2048, 2048], P('pipe', 'expert')
- grad_gate: bfloat16 [16, 16, 1024, 768], P('pipe', 'expert')
- grad_up: bfloat16 [16, 16, 1024, 768], P('pipe', 'expert')
- grad_down: bfloat16 [16, 16, 768, 1024], P('pipe', 'expert')
The draws below stay inside these ranges and needn't reach their ends.
Inputs may be any that keep to these rules, and one draw needn't show every extreme that they name: `route_ids`: each token names 2 different experts. Among the tokens of one device no expert is named by more than 32 of them, and in every draw the tokens of some device name some expert exactly 32 times.
All inputs are finite; a program needn't handle non-finite values.
Results may differ from the reference program's by a relative error of at most 0.0065.
Values may be sent and summed in bfloat16 or wider, within the bound.
No kernel may reach another device: no remote copies, remote signals or barrier semaphores. Data moves between devices by JAX's collectives and lax.ppermute only.
A program may use at most 128 MiB of HBM per device.

```python
import math
import jax
import jax.numpy as jnp
import numpy as np
from jax import lax

D = 2048
H = 768
TOPK = 2
TOK_DEV = 128
EXPERTS = 16
TOKENS = 2048
CAP = 32
N_PIPE = 16
N_EXPERT = 16


def block_levels(own_key, extent, cuts, smallest, top_value):
    gain, own = 1.0, jax.random.fold_in(own_key, 6)
    for dim, parts in cuts:
        draws = jnp.exp(jax.random.uniform(jax.random.fold_in(own, dim), (parts,), jnp.float32, smallest / len(cuts), top_value / len(cuts)))
        gain = gain * jnp.repeat(draws, extent[dim] // parts).reshape([-1 if axis == dim else 1 for axis in range(len(extent))])
    return gain


def deal_out(own_key, own, number, rows, number_of, top, reach, skew):
    sequence = jax.random.permutation(own_key, number_of)
    crowded, ordinary = portions_of(number_of, rows * top, reach, skew, True), portions_of(number_of, rows * top, reach, skew, False)
    places = jnp.arange(number_of)

    def named(sizes, rotation):
        used = int((sizes > 0).sum())
        fixed = max(1, used // 4)
        moved = fixed + (places - fixed + rotation * (used - fixed)) % max(1, number_of - fixed)
        return jnp.zeros((number_of,), jnp.int32).at[sequence[jnp.where(places < fixed, places, moved)]].set(jnp.asarray(sizes, jnp.int32))

    sizes = jnp.where(number % 4 == 0, named(crowded, number // 4), named(ordinary, number - number // 4 - 1))
    mixed = jax.random.permutation(jax.random.fold_in(own, 3), number_of)
    donor, sink = mixed[0:number_of // 2 * 2:2], mixed[1:number_of // 2 * 2:2]
    slack = jnp.minimum(sizes[donor] - 1, reach - sizes[sink]) // 2
    slack = jnp.where((donor == sequence[0]) | (sink == sequence[0]) | (sizes[sink] == 0), 0, jnp.maximum(slack, 0))
    moved = jax.random.randint(jax.random.fold_in(own, 4), (number_of // 2,), 0, 1 << 20) % (slack + 1)
    sizes = sizes.at[donor].add(-moved).at[sink].add(moved)
    items = jnp.searchsorted(jnp.cumsum(sizes), jnp.arange(rows * top), side="right").astype(jnp.int32)
    listing = items.reshape(top, rows).T
    listing = listing[jax.random.permutation(jax.random.fold_in(own, 1), rows)]
    rotation = jax.random.randint(jax.random.fold_in(own, 2), (rows, 1), 0, top)
    return jnp.take_along_axis(listing, (jnp.arange(top)[None, :] + rotation) % top, axis=1)


def portions_of(number_of, total, bound, skew, full):
    weights = [(1 << 20) // math.isqrt(grade ** skew) + 1 for grade in range(1, number_of + 1)]
    largest = bound if full else min(bound, max(-(-total // number_of), total * weights[0] // sum(weights)))
    least = 1 if total - largest >= number_of - 1 else 0
    holding, rest = [largest] + [least] * (number_of - 1), total - largest - least * (number_of - 1)
    while rest > 0:
        candidates = [i for i in range(1, number_of) if holding[i] < largest] or [i for i in range(1, number_of) if holding[i] < bound]
        whole, remaining = sum([weights[i] for i in candidates]), rest
        for i in candidates:
            extra = min(bound - holding[i], max(1, remaining * weights[i] // whole), rest)
            holding[i] = holding[i] + extra
            rest = rest - extra
    return np.array(holding)


def normal_values(rng, shape, spread, limit, split=(), held_as=jnp.bfloat16):
    array = jax.random.normal(rng, shape, jnp.float32) * spread
    if len(split) > 0:
        array = block_levels(rng, shape, split, -0.22, 0.18) * array
    return jnp.clip(array, min=-limit, max=limit).astype(held_as)


def setup_inputs(seed: int = 0) -> dict:
    streams_of = jax.random.split(jax.random.key(seed), 8)
    tokens = normal_values(streams_of[0], (N_PIPE, TOKENS, D), 1.0, 6.0, ((0, 16), (1, 16)))
    grad_out = normal_values(streams_of[1], (N_PIPE, TOKENS, D), 1.0, 6.0, ((0, 16), (1, 16)))
    route_ids_keys = jax.random.split(jax.random.fold_in(streams_of[2], 1), N_PIPE * TOKENS // TOK_DEV)
    route_ids_turns = jax.random.permutation(jax.random.fold_in(streams_of[2], 3), N_PIPE * TOKENS // TOK_DEV)
    route_ids = jax.vmap(lambda own, number: deal_out(jax.random.fold_in(streams_of[2], 2), own, number, TOK_DEV, EXPERTS, TOPK, CAP, 2))(route_ids_keys, route_ids_turns).reshape((N_PIPE, TOKENS, TOPK))
    route_probs = jnp.clip(0.1 + 0.9 * jax.random.uniform(streams_of[3], (N_PIPE, TOKENS, TOPK), jnp.float32) ** block_levels(streams_of[3], (N_PIPE, TOKENS, TOPK), ((0, 16), (1, 16)), -0.2, 0.2), 0.1, 1.0)
    w_gate = normal_values(streams_of[4], (N_PIPE, EXPERTS, D // 2, H), D ** -0.5, 0.125, ((0, 16), (1, 16)))
    w_up = normal_values(streams_of[5], (N_PIPE, EXPERTS, D // 2, H), D ** -0.5, 0.125, ((0, 16), (1, 16)))
    w_down = normal_values(streams_of[6], (N_PIPE, EXPERTS, H, D // 2), H ** -0.5, 0.21875, ((0, 16), (1, 16)))
    return dict(tokens=tokens, grad_out=grad_out, route_ids=route_ids, route_probs=route_probs, w_gate=w_gate, w_up=w_up, w_down=w_down)


def expert_pass(x_rows, dy_rows, inner, down):
    pre_act = jnp.dot(x_rows, inner, preferred_element_type=jnp.float32)
    gate_pre = pre_act[:, :H]
    up_pre = pre_act[:, H:]
    sigmoid_gate = jax.nn.sigmoid(gate_pre)
    silu_gate = gate_pre * sigmoid_gate
    hidden_act = (silu_gate * up_pre).astype(jnp.bfloat16)
    grad_hidden = jnp.dot(dy_rows, down.T, preferred_element_type=jnp.float32)
    grad_gate_pre = (grad_hidden * up_pre * sigmoid_gate * (1.0 + gate_pre * (1.0 - sigmoid_gate))).astype(jnp.bfloat16)
    grad_up_pre = (grad_hidden * silu_gate).astype(jnp.bfloat16)
    grad_pre = jnp.concatenate([grad_gate_pre, grad_up_pre], axis=1)
    contrib = jnp.dot(grad_pre, inner.T, preferred_element_type=jnp.float32).astype(jnp.bfloat16)
    inner_grad = jnp.dot(x_rows.T, grad_pre, preferred_element_type=jnp.float32).astype(jnp.bfloat16)
    down_grad = jnp.dot(hidden_act.T, dy_rows, preferred_element_type=jnp.float32).astype(jnp.bfloat16)
    return contrib, inner_grad, down_grad


def replica_pass(inputs, out_grads, route_rows, prob_rows, inner_full, down_full):
    rows_max = N_EXPERT * CAP

    def per_expert(total_grad, packed):
        expert, inner, down = packed
        matches = route_rows == expert
        routed = jnp.any(matches, axis=1)
        coefficient = jnp.sum(jnp.where(matches, prob_rows, 0.0), axis=1)
        row_index = jnp.nonzero(routed, size=rows_max, fill_value=0)[0].astype(jnp.int32)
        live_rows = (jnp.arange(rows_max, dtype=jnp.int32) < jnp.sum(routed.astype(jnp.int32)))[:, None]
        x_rows = jnp.where(live_rows, inputs[row_index], jnp.zeros((), inputs.dtype))
        scaled = out_grads[row_index].astype(jnp.float32) * coefficient[row_index][:, None]
        dy_rows = jnp.where(live_rows, scaled, 0.0).astype(jnp.bfloat16)
        contrib, inner_grad, down_grad = expert_pass(x_rows, dy_rows, inner, down)
        total_grad = total_grad.at[row_index].add(jnp.where(live_rows, contrib.astype(jnp.float32), 0.0))
        return total_grad, (inner_grad, down_grad)

    start = jnp.zeros((TOKENS, D), jnp.float32)
    total_grad, (inner_grads, down_grads) = lax.scan(per_expert, start, (jnp.arange(EXPERTS, dtype=jnp.int32), inner_full, down_full))
    return total_grad.astype(jnp.bfloat16), inner_grads, down_grads


def reference(tokens, grad_out, route_ids, route_probs, w_gate, w_up, w_down):
    half_pipes = N_PIPE // 2
    half_width = D // 2
    token_grads = [None] * N_PIPE
    gate_out = [None] * N_PIPE
    up_out = [None] * N_PIPE
    down_out = [None] * N_PIPE
    for layer_index in range(half_pipes):
        second = layer_index + half_pipes
        gate_full = jnp.concatenate([w_gate[layer_index], w_gate[second]], axis=1)
        up_full = jnp.concatenate([w_up[layer_index], w_up[second]], axis=1)
        inner_full = jnp.concatenate([gate_full, up_full], axis=2)
        down_full = jnp.concatenate([w_down[layer_index], w_down[second]], axis=2)
        inner_sum = jnp.zeros((EXPERTS, D, 2 * H), jnp.float32)
        down_sum = jnp.zeros((EXPERTS, H, D), jnp.float32)
        for pipe_index in (layer_index, second):
            grads_here, inner_grads, down_grads = replica_pass(tokens[pipe_index], grad_out[pipe_index], route_ids[pipe_index], route_probs[pipe_index], inner_full, down_full)
            token_grads[pipe_index] = grads_here
            inner_sum = inner_sum + inner_grads.astype(jnp.float32)
            down_sum = down_sum + down_grads.astype(jnp.float32)
        inner_sum = inner_sum.astype(jnp.bfloat16)
        down_sum = down_sum.astype(jnp.bfloat16)
        for block, pipe_index in ((0, layer_index), (1, second)):
            rows = inner_sum[:, block * half_width:(block + 1) * half_width, :]
            gate_out[pipe_index] = rows[:, :, :H]
            up_out[pipe_index] = rows[:, :, H:]
            down_out[pipe_index] = down_sum[:, :, block * half_width:(block + 1) * half_width]
    return (jnp.stack(token_grads), jnp.stack(gate_out), jnp.stack(up_out), jnp.stack(down_out))
```

```python
import functools

import jax
import jax.numpy as jnp
from jax import lax
from jax.experimental import pallas as pl
from jax.experimental.pallas import tpu as pltpu
from jax.sharding import PartitionSpec as P

BF = jnp.bfloat16
F32 = jnp.float32
LANES = 128
TILE = 256
VMEM = pl.BlockSpec(memory_space=pltpu.VMEM)
SMEM = pl.BlockSpec(memory_space=pltpu.SMEM)
HBM = pl.BlockSpec(memory_space=pltpu.HBM)
ANY = pl.BlockSpec(memory_space=pl.ANY)


def call(kernel, outs, ins, name, after=(), scratch=(), copies=0, vmem=16, **more):
    ins = [a if isinstance(a, tuple) else (a, HBM) for a in ins]
    outs = [o if isinstance(o[1], pl.BlockSpec) else (o, HBM) for o in outs]
    count = len(ins)
    after = [a[0] if isinstance(a, tuple) else pinned(a) for a in after]

    def body(*refs):
        kernel(*refs[:count], *refs[count + len(after) :])

    return pl.pallas_call(
        body,
        out_shape=[pltpu.HBM(*o) for o, _ in outs],
        in_specs=[s for _, s in ins] + [ANY] * len(after),
        out_specs=[s for _, s in outs],
        scratch_shapes=list(scratch) + [pltpu.SemaphoreType.DMA((max(copies, 1),))],
        name=name,
        cost_estimate=pl.CostEstimate(
            flops=0, bytes_accessed=0, transcendentals=0
        ),
        compiler_params=pltpu.CompilerParams(vmem_limit_bytes=vmem * 2**20),
        **more,
    )(*[a if spec in (ANY, SMEM, VMEM) else pinned(a) for a, spec in ins], *after)


def pinned(a):
    if a.size * a.dtype.itemsize < 512:
        return a
    return pltpu.with_memory_space_constraint(a, pltpu.HBM)


def columns(rows, width, offset=0):
    return pl.BlockSpec((rows, width), lambda i: (0, i + offset))


class Copies:
    def __init__(self, sems):
        self.sems, self.made = sems, []

    def start(self, source, target):
        copy = pltpu.make_async_copy(source, target, self.sems.at[len(self.made)])
        copy.start()
        self.made.append(copy)
        return copy


def dot(a, b, contract):
    return lax.dot_general(
        a, b, ((contract[:1], contract[1:]), ((), ())), preferred_element_type=F32
    )


def pack_kernel(
    block_ref, tok_ref, grad_ref, ids_ref, probs_ref, own_ref, other_ref, sems
):
    half = tok_ref.shape[1] // 2
    first = block_ref[0] == 0
    for ref, at in ((tok_ref, 0), (grad_ref, half)):
        left, right = ref[:, :half], ref[:, half:]
        own_ref[:, at : at + half] = jnp.where(first, left, right)
        other_ref[:, at : at + half] = jnp.where(first, right, left)
    rest = probs_ref[...]
    parts = [ids_ref[...].astype(F32)]
    for _ in range(3):
        piece = rest.astype(BF).astype(F32)
        parts.append(piece)
        rest = rest - piece
    line = lax.broadcasted_iota(jnp.int32, (LANES, rest.shape[1]), 0)
    info = jnp.zeros(line.shape, F32)
    for n, part in enumerate(parts):
        for k in range(2):
            info = jnp.where(line == 2 * n + k, part[k : k + 1], info)
    info = info.T
    own_ref[:, 2 * half :] = info.astype(BF)
    other_ref[:, 2 * half :] = info.astype(BF)


def choose(members, info, chosen_ref, scale_ref):
    count = info.shape[1]
    capacity = chosen_ref.shape[0] // members.shape[0]
    match0 = members == info[0:1]
    match1 = members == info[1:2]
    prob0 = info[2:3] + info[4:5] + info[6:7]
    prob1 = info[3:4] + info[5:6] + info[7:8]
    routed = jnp.where(match0 | match1, 1.0, 0.0)
    coefficient = jnp.where(match0, prob0, 0.0) + jnp.where(match1, prob1, 0.0)
    earlier = lax.broadcasted_iota(jnp.int32, (count, count), 0)
    later = lax.broadcasted_iota(jnp.int32, (count, count), 1)
    before = jnp.where(earlier < later, 1.0, 0.0).astype(BF)
    slot = dot(routed.astype(BF), before, (1, 0))
    slot = jnp.where(routed > 0.5, slot, -1.0)
    ids = lax.broadcasted_iota(jnp.int32, (capacity, count), 0).astype(F32)
    for m in range(members.shape[0]):
        at = pl.ds(m * capacity, capacity)
        hit = ids == slot[m : m + 1]
        chosen_ref[at, :] = jnp.where(hit, 1.0, 0.0).astype(BF)
        scale_ref[at, :] = jnp.sum(
            jnp.where(hit, coefficient[m : m + 1], 0.0), axis=1, keepdims=True
        )


def gather_kernel(members_ref, own_ref, other_ref, *refs):
    parts, sent_refs, chosen_refs = 4, refs[:4], refs[4:6]
    loads, sent, chosens, scale, sems = refs[6:8], refs[8], refs[9:11], refs[11], refs[12]
    half = sent.shape[1] // 2
    capacity = sent.shape[0] // (2 * parts)
    copies = Copies(sems)
    first, second = slice(0, half), slice(half, 2 * half)
    info_at = slice(2 * half, 2 * half + LANES)
    ready = [
        [copies.start(ref.at[:, at], load.at[:, at]) for at in (info_at, first, second)]
        for ref, load in ((own_ref, loads[0]), (other_ref, loads[1]))
    ]
    out = []
    for n in range(2):
        ready[n][0].wait()
        info = loads[n][:, info_at].astype(F32).T
        choose(members_ref[...], info, chosens[n], scale.at[n])
        out.append(copies.start(chosens[n], chosen_refs[n]))
    for m, at in enumerate((first, second)):
        for n in range(2):
            ready[n][m + 1].wait()
            picked = dot(chosens[n][...], loads[n][:, at], (1, 0))
            if m:
                picked = picked * scale[n]
            picked = picked.astype(BF)
            for k in range(parts):
                row = (2 * k + n) * capacity
                sent[row : row + capacity, at] = picked[
                    k * capacity : (k + 1) * capacity
                ]
        for k in range(parts):
            rows = slice(2 * k * capacity, 2 * (k + 1) * capacity)
            out.append(copies.start(sent.at[rows, at], sent_refs[k].at[:, at]))
    for copy in out:
        copy.wait()


def forward_kernel(*refs):
    item_refs, (gate_ref, up_ref, down_ref) = refs[:4], refs[4:7]
    sent_ref, whole_ref, items, gate, up, down, sent, sems = refs[7:]
    half, hidden = gate.shape
    copies = Copies(sems)
    first, second = slice(0, half), slice(half, 2 * half)
    size = items.shape[0] // len(item_refs)

    def fetch(at):
        return [
            copies.start(ref.at[:, at], items.at[k * size : (k + 1) * size, at])
            for k, ref in enumerate(item_refs)
        ]

    x_in = fetch(first)
    gate_in = copies.start(gate_ref, gate)
    up_in = copies.start(up_ref, up)
    dy_in = fetch(second)
    down_in = copies.start(down_ref, down)
    out = []
    for n, (ready, cols, w, contract) in enumerate(
        (
            (x_in + [gate_in], first, gate, (1, 0)),
            ([up_in], first, up, (1, 0)),
            (dy_in + [down_in], second, down, (1, 1)),
        )
    ):
        for copy in ready:
            copy.wait()
        at = slice(n * hidden, (n + 1) * hidden)
        sent[:, at] = dot(items[:, cols], w[...], contract).astype(BF)
        out.append(copies.start(sent.at[:, at], sent_ref.at[:, at]))
    out.append(copies.start(items, whole_ref))
    for copy in out:
        copy.wait()


def backward_kernel(*refs):
    mine_ref, theirs_ref, gate_ref, up_ref, d_ref = refs[:5]
    contrib_refs = refs[5:9]
    mine, theirs, gate, up, d, contrib, sems = refs[9:]
    half, hidden = gate.shape
    rows = mine.shape[0]
    copies = Copies(sems)
    step = rows // 4
    size = rows // len(contrib_refs)
    parts = []
    for r in range(0, rows, step):
        at = slice(r, r + step)
        parts.append(
            (
                copies.start(mine_ref.at[at], mine.at[at]),
                copies.start(theirs_ref.at[at], theirs.at[at]),
            )
        )
    gate_in = copies.start(gate_ref, gate)
    up_in = copies.start(up_ref, up)
    out = []
    for n, pair in enumerate(parts):
        at = slice(n * step, (n + 1) * step)
        for copy in pair:
            copy.wait()
        g, u, dh = [
            mine[at, m * hidden : (m + 1) * hidden].astype(F32)
            + theirs[at, m * hidden : (m + 1) * hidden].astype(F32)
            for m in range(3)
        ]
        sig = jax.nn.sigmoid(g)
        silu = g * sig
        d[at, :hidden] = (dh * u * sig * (1.0 + g * (1.0 - sig))).astype(BF)
        d[at, hidden : 2 * hidden] = (dh * silu).astype(BF)
        d[at, 2 * hidden :] = (silu * u).astype(BF)
        out.append(copies.start(d.at[at], d_ref.at[at]))
    gate_in.wait()
    up_in.wait()
    for n in range(2):
        at = slice(n * half // 2, (n + 1) * half // 2)
        contrib[:, at] = (
            dot(d[:, :hidden], gate[at, :], (1, 1))
            + dot(d[:, hidden : 2 * hidden], up[at, :], (1, 1))
        ).astype(BF)
        for k, ref in enumerate(contrib_refs):
            part = contrib.at[k * size : (k + 1) * size, at]
            out.append(copies.start(part, ref.at[:, at]))
    for copy in out:
        copy.wait()


def combine_kernel(*refs):
    chosen_refs, got_refs, out_refs, (got, sems) = refs[:2], refs[2:6], refs[6:8], refs[8:]
    copies = Copies(sems)
    capacity = got_refs[0].shape[0] // 2
    ready = [
        [
            copies.start(
                ref.at[n * capacity : (n + 1) * capacity],
                got.at[n, k * capacity : (k + 1) * capacity],
            )
            for k, ref in enumerate(got_refs)
        ]
        for n in (1, 0)
    ]
    for n, parts in zip((1, 0), ready):
        for copy in parts:
            copy.wait()
        out_refs[n][...] = dot(chosen_refs[n][...], got[n], (0, 0)).astype(BF)


def finish_kernel(block_ref, a_ref, b_ref, c_ref, rest_ref, out_ref, sems):
    half = a_ref.shape[1]
    kept = sum(ref[...].astype(F32) for ref in (a_ref, b_ref, c_ref)).astype(BF)
    rest = rest_ref[...]
    first = block_ref[0] == 0
    out_ref[:, :half] = jnp.where(first, kept, rest)
    out_ref[:, half:] = jnp.where(first, rest, kept)


def grads_kernel(pairs, *refs):
    item_refs, d_refs = refs[:pairs], refs[pairs : 2 * pairs]
    old_refs, new_refs = refs[2 * pairs : -4], refs[-4:-1]
    tile, hidden = new_refs[0].shape
    half = item_refs[0].shape[1] // 2
    base = pl.multiple_of(pl.program_id(0) * tile, tile)

    def write(n, value):
        value = value.astype(BF)
        if old_refs:
            value = (old_refs[n][...].astype(F32) + value.astype(F32)).astype(BF)
        new_refs[n][...] = value

    for n in range(2):
        at = slice(n * hidden, (n + 1) * hidden)
        write(
            n,
            sum(
                dot(x[:, pl.ds(base, tile)], d[:, at], (0, 0))
                for x, d in zip(item_refs, d_refs)
            ),
        )
    outer = sum(
        dot(y[:, pl.ds(base + half, tile)], d[:, 2 * hidden :], (0, 0))
        for y, d in zip(item_refs, d_refs)
    )
    write(2, outer.T)


def local(tokens, grad_out, route_ids, route_probs, w_gate, w_up, w_down):
    pipes = lax.axis_size("pipe")
    experts = lax.axis_size("expert")
    block = lax.axis_index("pipe") // (pipes // 2)
    block = jnp.asarray(block, jnp.int32).reshape(1)
    plane = lax.axis_index("expert") // 2 % 2
    count, width = tokens.shape[1:]
    half, hidden = w_gate.shape[2:]
    capacity = 2 * count * route_ids.shape[2] // experts
    chips = experts // 4
    rows = experts * capacity // 2
    gate, up, down = w_gate[0, 0], w_up[0, 0], w_down[0, 0]

    peers = [(i, (i + pipes // 2) % pipes) for i in range(pipes)]
    planes = [(e, e ^ 2) for e in range(experts)]
    cores = [(e, e ^ 1) for e in range(experts)]
    across = [
        (p * experts + e, q * experts + f) for p, q in peers for e, f in cores
    ]
    turns = [[(e, (e + 4 * k) % experts) for e in range(experts)] for k in range(chips)]
    backs = [[(f, e) for e, f in turn] for turn in turns]
    here = lax.axis_index("expert")
    members = (here + 4 * jnp.arange(chips, dtype=jnp.int32)) % experts
    members = members.astype(F32)[:, None]

    def spread(parts, routes):
        moved = [lax.ppermute(a, "expert", r) for a, r in zip(parts[1:], routes[1:])]
        return [parts[0]] + moved

    def whole(a):
        return a, pl.BlockSpec(a.shape)

    def whole_out(*shape):
        return (shape, BF), pl.BlockSpec(shape)

    packed = whole_out(count, width + LANES)
    own, swapped = call(
        pack_kernel,
        [packed, packed],
        [(block, SMEM)]
        + [
            whole(a)
            for a in (tokens[0], grad_out[0], route_ids[0].T, route_probs[0].T)
        ],
        "pack",
    )
    load = {"ol": own}
    partner = {"ol": "sl", "sl": "ol", "oz": "sz", "sz": "oz"}
    chosen, pieces, items, theirs, d, got, outgoing, other = ({} for _ in range(8))

    def buffers(*shapes):
        return [pltpu.VMEM(s, BF) for s in shapes]

    def gather(k, *after):
        out = call(
            gather_kernel,
            [((2 * capacity, width), BF)] * chips + [((rows // 2, count), BF)] * 2,
            [whole(members), load[k] if k == "ol" else (load[k], ANY), (other[k], ANY)],
            "gather_" + k,
            after,
            buffers(
                (count, width + LANES),
                (count, width + LANES),
                (rows, width),
                (rows // 2, count),
                (rows // 2, count),
            )
            + [pltpu.VMEM((2, rows // 2, 1), F32)],
            16,
        )
        chosen[k] = out[chips:]
        pieces[k] = spread(out[:chips], turns)
        return out[0]

    def forward(k, *after):
        outgoing[k], items[k] = call(
            forward_kernel,
            [((rows, 3 * hidden), BF), ((rows, width), BF)],
            [pieces[k][0]] + [(a, ANY) for a in pieces[k][1:]] + [gate, up, down],
            "forward_" + k,
            after,
            buffers(
                (rows, width),
                (half, hidden),
                (half, hidden),
                (hidden, half),
                (rows, 3 * hidden),
            ),
            16,
        )
        return outgoing[k]

    def swap(k, *after):
        out, *_ = lax.optimization_barrier((outgoing[k], *after))
        theirs[partner[k]] = lax.ppermute(out, "pipe", peers)

    def join(k, *after):
        mine, *_ = lax.optimization_barrier((load[k], *after))
        other[k] = lax.ppermute(mine, "expert", cores)

    def backward(k, *after):
        out = call(
            backward_kernel,
            [((rows, 3 * hidden), BF)] + [((2 * capacity, half), BF)] * chips,
            [outgoing[k], (theirs[k], ANY), gate, up],
            "backward_" + k,
            after,
            buffers(
                (rows, 3 * hidden),
                (rows, 3 * hidden),
                (half, hidden),
                (half, hidden),
                (rows, 3 * hidden),
                (rows, half),
            ),
            24,
        )
        d[k] = out[0]
        got[k] = spread(out[1:], backs)
        return d[k]

    def combine(k, *after):
        mine, other = call(
            combine_kernel,
            [whole_out(count, half)] * 2,
            [whole(a) for a in chosen[k]] + [got[k][0]] + [(a, ANY) for a in got[k][1:]],
            "combine_" + k,
            after,
            buffers((2, rows // 2, half)),
            8,
        )
        return mine, lax.ppermute(other, "expert", cores)

    def added(*parts):
        return sum(a.astype(F32) for a in parts).astype(BF)

    rowwise = pl.BlockSpec((TILE, hidden), lambda i: (i, 0))
    grad_specs = [rowwise, rowwise, columns(hidden, TILE)]
    grad_types = [((half, hidden), BF), ((half, hidden), BF), ((hidden, half), BF)]

    def weight_grads(pair, old, *after):
        return call(
            functools.partial(grads_kernel, len(pair)),
            list(zip(grad_types, grad_specs)),
            [(a, pl.BlockSpec(a.shape, lambda i: (0, 0))) for a in
             [items[k] for k in pair] + [d[k] for k in pair]]
            + list(zip(old, grad_specs)),
            "grads_" + pair[0],
            after,
            vmem=40,
            grid=(half // TILE,),
        )

    load["oz"] = lax.ppermute(own, "expert", planes)
    load["sl"] = lax.ppermute(swapped, "pipe", peers)
    load["sz"] = lax.ppermute(load["sl"], "expert", planes)
    join("ol")
    t = gather("ol")
    other["sl"] = lax.ppermute(swapped, ("pipe", "expert"), across)
    t = gather("sl", t)
    t = forward("ol", t)
    swap("ol")
    join("oz", t)
    t = gather("oz", t)
    t = forward("sl", t)
    t = forward("oz", t)
    swap("oz")
    join("sz", t)
    t = gather("sz", t)
    t = backward("sl", t)
    t = forward("sz", t)
    swap("sz")
    t = backward("sz", t)
    swap("sl", t)
    sz = combine("sz", t)
    extra_other = lax.ppermute(added(*sz), "expert", planes)
    t = backward("oz", sz[0])
    sl = combine("sl", t)
    half_grads = weight_grads(("sl", "sz"), [], sl[0])
    oz = combine("oz", half_grads[0])
    extra_own = lax.ppermute(added(*oz), "expert", planes)
    rest = lax.ppermute(added(*sl, extra_other), "pipe", peers)
    t = backward("ol", oz[0])
    grads = weight_grads(("ol", "oz"), half_grads, t, (extra_own,), (rest,))
    ol = combine("ol", grads[0])
    (token_grad,) = call(
        finish_kernel,
        [whole_out(count, width)],
        [(block, SMEM)]
        + [whole(ol[0])] + [(a, VMEM) for a in (ol[1], extra_own, rest)],
        "finish",
    )
    return (token_grad[None],) + tuple(g[None, None] for g in grads)


def solution(mesh):
    rank3 = P("pipe", "expert", None)
    rank4 = P("pipe", "expert", None, None)
    return jax.shard_map(
        local,
        mesh=mesh,
        in_specs=(rank3,) * 4 + (rank4,) * 3,
        out_specs=(rank3, rank4, rank4, rank4),
        check_vma=False,
    )
```

```python
import functools

import jax
import jax.numpy as jnp
from jax import lax
from jax.experimental import pallas as pl
from jax.experimental.pallas import tpu as pltpu
from jax.sharding import PartitionSpec as P

BF = jnp.bfloat16
F32 = jnp.float32
LANES = 128
TILE = 256
VMEM = pl.BlockSpec(memory_space=pltpu.VMEM)
SMEM = pl.BlockSpec(memory_space=pltpu.SMEM)
HBM = pl.BlockSpec(memory_space=pltpu.HBM)
ANY = pl.BlockSpec(memory_space=pl.ANY)


def call(kernel, outs, ins, name, after=(), scratch=(), copies=0, vmem=16, **more):
    ins = [a if isinstance(a, tuple) else (a, HBM) for a in ins]
    outs = [o if isinstance(o[1], pl.BlockSpec) else (o, HBM) for o in outs]
    count = len(ins)
    after = [a[0] if isinstance(a, tuple) else pinned(a) for a in after]

    def body(*refs):
        kernel(*refs[:count], *refs[count + len(after) :])

    return pl.pallas_call(
        body,
        out_shape=[
            (jax.ShapeDtypeStruct if spec is VMEM else pltpu.HBM)(*o) for o, spec in outs
        ],
        in_specs=[s for _, s in ins] + [ANY] * len(after),
        out_specs=[s for _, s in outs],
        scratch_shapes=list(scratch) + [pltpu.SemaphoreType.DMA((max(copies, 1),))],
        name=name,
        cost_estimate=pl.CostEstimate(
            flops=0, bytes_accessed=0, transcendentals=0
        ),
        compiler_params=pltpu.CompilerParams(vmem_limit_bytes=vmem * 2**20),
        **more,
    )(*[a if spec in (ANY, SMEM, VMEM) else pinned(a) for a, spec in ins], *after)


def pinned(a):
    if a.size * a.dtype.itemsize < 512:
        return a
    return pltpu.with_memory_space_constraint(a, pltpu.HBM)


def columns(rows, width, offset=0):
    return pl.BlockSpec((rows, width), lambda i: (0, i + offset))


class Copies:
    def __init__(self, sems):
        self.sems, self.made = sems, []

    def start(self, source, target):
        copy = pltpu.make_async_copy(source, target, self.sems.at[len(self.made)])
        copy.start()
        self.made.append(copy)
        return copy


def dot(a, b, contract):
    return lax.dot_general(
        a, b, ((contract[:1], contract[1:]), ((), ())), preferred_element_type=F32
    )


def pack_kernel(
    block_ref, tok_ref, grad_ref, ids_ref, probs_ref, own_ref, other_ref, sems
):
    half = tok_ref.shape[1] // 2
    first = block_ref[0] == 0
    for ref, at in ((tok_ref, 0), (grad_ref, half)):
        left, right = ref[:, :half], ref[:, half:]
        own_ref[:, at : at + half] = jnp.where(first, left, right)
        other_ref[:, at : at + half] = jnp.where(first, right, left)
    rest = probs_ref[...]
    parts = [ids_ref[...].astype(F32)]
    for _ in range(3):
        piece = rest.astype(BF).astype(F32)
        parts.append(piece)
        rest = rest - piece
    line = lax.broadcasted_iota(jnp.int32, (LANES, rest.shape[1]), 0)
    info = jnp.zeros(line.shape, F32)
    for n, part in enumerate(parts):
        for k in range(2):
            info = jnp.where(line == 2 * n + k, part[k : k + 1], info)
    info = info.T
    own_ref[:, 2 * half :] = info.astype(BF)
    other_ref[:, 2 * half :] = info.astype(BF)


def choose(members, info, chosen_ref, scale_ref):
    count = info.shape[1]
    capacity = chosen_ref.shape[0] // members.shape[0]
    match0 = members == info[0:1]
    match1 = members == info[1:2]
    prob0 = info[2:3] + info[4:5] + info[6:7]
    prob1 = info[3:4] + info[5:6] + info[7:8]
    routed = jnp.where(match0 | match1, 1.0, 0.0)
    coefficient = jnp.where(match0, prob0, 0.0) + jnp.where(match1, prob1, 0.0)
    earlier = lax.broadcasted_iota(jnp.int32, (count, count), 0)
    later = lax.broadcasted_iota(jnp.int32, (count, count), 1)
    before = jnp.where(earlier < later, 1.0, 0.0).astype(BF)
    slot = dot(routed.astype(BF), before, (1, 0))
    slot = jnp.where(routed > 0.5, slot, -1.0)
    ids = lax.broadcasted_iota(jnp.int32, (capacity, count), 0).astype(F32)
    for m in range(members.shape[0]):
        at = pl.ds(m * capacity, capacity)
        hit = ids == slot[m : m + 1]
        chosen_ref[at, :] = jnp.where(hit, 1.0, 0.0).astype(BF)
        scale_ref[at, :] = jnp.sum(
            jnp.where(hit, coefficient[m : m + 1], 0.0), axis=1, keepdims=True
        )


def gather_kernel(chunks, members_ref, *refs):
    n_loads, parts = 2 * chunks, 4
    load_refs, sent_refs = refs[:n_loads], refs[n_loads : n_loads + parts]
    chosen_refs = refs[n_loads + parts : 2 * n_loads + parts]
    loads, sent, chosens, scale, sems = refs[2 * n_loads + parts :]
    half = sent.shape[1] // 2
    capacity = sent.shape[0] // (n_loads * parts)
    copies = Copies(sems)
    first, second = slice(0, half), slice(half, 2 * half)
    info_at = slice(2 * half, 2 * half + LANES)
    ready = [
        [
            copies.start(ref.at[:, at], loads.at[n, :, at])
            for at in (info_at, first, second)
        ]
        for n, ref in enumerate(load_refs)
    ]
    out = []
    for n in range(n_loads):
        ready[n][0].wait()
        info = loads[n, :, info_at].astype(F32).T
        choose(members_ref[...], info, chosens.at[n], scale.at[n])
        out.append(copies.start(chosens.at[n], chosen_refs[n]))
    for m, at in enumerate((first, second)):
        for n in range(n_loads):
            ready[n][m + 1].wait()
            picked = dot(chosens[n], loads[n, :, at], (1, 0))
            if m:
                picked = picked * scale[n]
            picked = picked.astype(BF)
            for k in range(parts):
                row = (n_loads * k + n) * capacity
                sent[row : row + capacity, at] = picked[
                    k * capacity : (k + 1) * capacity
                ]
        for k in range(parts):
            rows = slice(n_loads * k * capacity, n_loads * (k + 1) * capacity)
            out.append(copies.start(sent.at[rows, at], sent_refs[k].at[:, at]))
    for copy in out:
        copy.wait()


def warm_kernel(gate_ref, up_ref, down_ref, out_ref, sems):
    out_ref[...] = jnp.zeros_like(out_ref)


def forward_kernel(offset, *refs):
    item_refs, (gate, up, down) = refs[:4], refs[4:7]
    sent_ref, whole_ref, items, sent, sems = refs[7:]
    half, hidden = gate.shape
    copies = Copies(sems)
    first, second = slice(0, half), slice(half, 2 * half)
    size = items.shape[0] // len(item_refs)
    held = slice(offset * size, (offset + 1) * size)

    def fetch(at):
        return [
            copies.start(ref.at[held, at], items.at[k * size : (k + 1) * size, at])
            for k, ref in enumerate(item_refs)
        ]

    x_in = fetch(first)
    dy_in = fetch(second)
    out = []
    for n, (ready, cols, w, contract) in enumerate(
        (
            (x_in, first, gate, (1, 0)),
            ([], first, up, (1, 0)),
            (dy_in, second, down, (1, 1)),
        )
    ):
        for copy in ready:
            copy.wait()
        at = slice(n * hidden, (n + 1) * hidden)
        sent[:, at] = dot(items[:, cols], w[...], contract).astype(BF)
        out.append(copies.start(sent.at[:, at], sent_ref.at[:, at]))
    out.append(copies.start(items, whole_ref))
    for copy in out:
        copy.wait()


def backward_kernel(chunks, *refs):
    mine_refs, theirs_refs = refs[:chunks], refs[chunks : 2 * chunks]
    gate, up = refs[2 * chunks : 2 * chunks + 2]
    d_refs = refs[2 * chunks + 2 : 3 * chunks + 2]
    contrib_refs = refs[3 * chunks + 2 : -5]
    mine, theirs, d, contrib, sems = refs[-5:]
    half, hidden = gate.shape
    rows = mine.shape[0] // chunks
    copies = Copies(sems)
    step = rows // 4
    size = rows // len(contrib_refs)
    parts = []
    for c in range(chunks):
        for r in range(0, rows, step):
            at, held = slice(r, r + step), slice(c * rows + r, c * rows + r + step)
            parts.append(
                (
                    copies.start(mine_refs[c].at[at], mine.at[held]),
                    copies.start(theirs_refs[c].at[at], theirs.at[held]),
                )
            )
    out = []
    for n, pair in enumerate(parts):
        at = slice(n * step, (n + 1) * step)
        for copy in pair:
            copy.wait()
        g, u, dh = [
            mine[at, m * hidden : (m + 1) * hidden].astype(F32)
            + theirs[at, m * hidden : (m + 1) * hidden].astype(F32)
            for m in range(3)
        ]
        sig = jax.nn.sigmoid(g)
        silu = g * sig
        d[at, :hidden] = (dh * u * sig * (1.0 + g * (1.0 - sig))).astype(BF)
        d[at, hidden : 2 * hidden] = (dh * silu).astype(BF)
        d[at, 2 * hidden :] = (silu * u).astype(BF)
        c, r = n // 4, n % 4 * step
        out.append(copies.start(d.at[at], d_refs[c].at[r : r + step]))
    for n in range(2):
        at = slice(n * half // 2, (n + 1) * half // 2)
        contrib[:, at] = (
            dot(d[:, :hidden], gate[at, :], (1, 1))
            + dot(d[:, hidden : 2 * hidden], up[at, :], (1, 1))
        ).astype(BF)
        for c in range(chunks):
            for k, ref in enumerate(contrib_refs):
                row = c * rows + k * size
                out.append(
                    copies.start(
                        contrib.at[row : row + size, at],
                        ref.at[c * size : (c + 1) * size, at],
                    )
                )
    for copy in out:
        copy.wait()


def combine_kernel(chunks, *refs):
    chosen_refs, got_refs = refs[: 2 * chunks], refs[2 * chunks : 2 * chunks + 4]
    own_refs, other_ref, got, sems = refs[2 * chunks + 4 : -3], *refs[-3:]
    copies = Copies(sems)
    capacity = got_refs[0].shape[0] // (2 * chunks)
    count = other_ref.shape[0] // chunks
    order = [(c, n) for n in (1, 0) for c in range(chunks)]
    ready = [
        [
            copies.start(
                ref.at[(2 * c + n) * capacity : (2 * c + n + 1) * capacity],
                got.at[2 * c + n, k * capacity : (k + 1) * capacity],
            )
            for k, ref in enumerate(got_refs)
        ]
        for c, n in order
    ]
    for (c, n), parts in zip(order, ready):
        for copy in parts:
            copy.wait()
        value = dot(chosen_refs[2 * c + n][...], got[2 * c + n], (0, 0)).astype(BF)
        if n:
            other_ref[c * count : (c + 1) * count] = value
        else:
            own_refs[c][...] = value


def finish_kernel(block_ref, a_ref, b_ref, c_ref, rest_ref, out_ref, sems):
    half = a_ref.shape[1]
    kept = sum(ref[...].astype(F32) for ref in (a_ref, b_ref, c_ref)).astype(BF)
    rest = rest_ref[...]
    first = block_ref[0] == 0
    out_ref[:, :half] = jnp.where(first, kept, rest)
    out_ref[:, half:] = jnp.where(first, rest, kept)


def grads_kernel(pairs, final, *refs):
    item_refs, d_refs = refs[:pairs], refs[pairs : 2 * pairs]
    old_refs, new_refs = refs[2 * pairs : -4], refs[-4:-1]
    hidden = new_refs[0].shape[1]
    half = item_refs[0].shape[1] // 2
    base = pl.multiple_of(pl.program_id(0) * TILE, TILE)
    tile = pl.ds(base, TILE)

    def write(n, value):
        at = (slice(None), tile) if n == 2 else (tile, slice(None))
        value = value.astype(BF)
        if final:
            value = (old_refs[n][at].astype(F32) + value.astype(F32)).astype(BF)
            new_refs[n][...] = value
        else:
            new_refs[n][at] = value

    for n in range(2):
        cols = slice(n * hidden, (n + 1) * hidden)
        write(
            n,
            sum(dot(x[:, tile], d[:, cols], (0, 0)) for x, d in zip(item_refs, d_refs)),
        )
    outer = sum(
        dot(y[:, pl.ds(base + half, TILE)], d[:, 2 * hidden :], (0, 0))
        for y, d in zip(item_refs, d_refs)
    )
    write(2, outer.T)


def local(tokens, grad_out, route_ids, route_probs, w_gate, w_up, w_down):
    pipes = lax.axis_size("pipe")
    experts = lax.axis_size("expert")
    block = lax.axis_index("pipe") // (pipes // 2)
    block = jnp.asarray(block, jnp.int32).reshape(1)
    plane = lax.axis_index("expert") // 2 % 2
    count, width = tokens.shape[1:]
    half, hidden = w_gate.shape[2:]
    capacity = 2 * count * route_ids.shape[2] // experts
    chips = experts // 4
    rows = experts * capacity // 2
    gate, up, down = w_gate[0, 0], w_up[0, 0], w_down[0, 0]

    peers = [(i, (i + pipes // 2) % pipes) for i in range(pipes)]
    planes = [(e, e ^ 2) for e in range(experts)]
    cores = [(e, e ^ 1) for e in range(experts)]
    turns = [[(e, (e + 4 * k) % experts) for e in range(experts)] for k in range(chips)]
    backs = [[(f, e) for e, f in turn] for turn in turns]
    here = lax.axis_index("expert")
    members = (here + 4 * jnp.arange(chips, dtype=jnp.int32)) % experts
    members = members.astype(F32)[:, None]

    def spread(parts, routes):
        moved = [lax.ppermute(a, "expert", r) for a, r in zip(parts[1:], routes[1:])]
        return [parts[0]] + moved

    def whole(a):
        return a, pl.BlockSpec(a.shape)

    def whole_out(*shape):
        return (shape, BF), pl.BlockSpec(shape)

    packed = whole_out(count, width + LANES)
    own, swapped = call(
        pack_kernel,
        [packed, packed],
        [(block, SMEM)]
        + [
            whole(a)
            for a in (tokens[0], grad_out[0], route_ids[0].T, route_probs[0].T)
        ],
        "pack",
    )
    load = {"ol": own}
    partner = {"ol": "sl", "sl": "ol", "oz": "sz", "sz": "oz"}
    chosen, pieces, items, theirs, d, got, outgoing, other = ({} for _ in range(8))

    weights = [(a, VMEM) for a in (gate, up, down)]

    def buffers(*shapes):
        return [pltpu.VMEM(s, BF) for s in shapes]

    def gather(keys, *after):
        n = len(keys)
        loads = [
            a if a is own else (a, ANY) for k in keys for a in (load[k], other[k])
        ]
        out = call(
            functools.partial(gather_kernel, n),
            [((2 * n * capacity, width), BF)] * chips
            + [((rows // 2, count), BF)] * (2 * n),
            [whole(members)] + loads,
            "gather_" + "_".join(keys),
            after,
            buffers(
                (2 * n, count, width + LANES),
                (n * rows, width),
                (2 * n, rows // 2, count),
            )
            + [pltpu.VMEM((2 * n, rows // 2, 1), F32)],
            8 * n + 8,
        )
        moved = spread(out[:chips], turns)
        for c, k in enumerate(keys):
            chosen[k] = out[chips + 2 * c : chips + 2 * c + 2]
            pieces[k] = c, moved
        return out[0]

    def forward(k, *after):
        offset, moved = pieces[k]
        outgoing[k], items[k] = call(
            functools.partial(forward_kernel, offset),
            [((rows, 3 * hidden), BF), ((rows, width), BF)],
            [moved[0]] + [(a, ANY) for a in moved[1:]] + weights,
            "forward_" + k,
            after,
            buffers((rows, width), (rows, 3 * hidden)),
            16,
        )
        return outgoing[k]

    def swap(k, *after):
        out, *_ = lax.optimization_barrier((outgoing[k], *after))
        theirs[partner[k]] = lax.ppermute(out, "pipe", peers)

    def join(k, *after):
        mine, *_ = lax.optimization_barrier((load[k], *after))
        other[k] = lax.ppermute(mine, "expert", cores)

    def backward(keys, *after):
        n = len(keys)
        out = call(
            functools.partial(backward_kernel, n),
            [((rows, 3 * hidden), BF)] * n + [((2 * n * capacity, half), BF)] * chips,
            [outgoing[k] for k in keys]
            + [(theirs[k], ANY) for k in keys]
            + weights[:2],
            "backward_" + "_".join(keys),
            after,
            buffers(
                (n * rows, 3 * hidden),
                (n * rows, 3 * hidden),
                (n * rows, 3 * hidden),
                (n * rows, half),
            ),
            20 * n + 2,
            vmem=24,
        )
        d.update(zip(keys, out))
        got[keys] = spread(out[n:], backs)
        return out[0]

    def combine(keys, *after):
        n = len(keys)
        *mine, partners = call(
            functools.partial(combine_kernel, n),
            [whole_out(count, half)] * n + [whole_out(n * count, half)],
            [whole(a) for k in keys for a in chosen[k]]
            + [got[keys][0]]
            + [(a, ANY) for a in got[keys][1:]],
            "combine_" + "_".join(keys),
            after,
            buffers((2 * n, rows // 2, half)),
            8 * n,
        )
        moved = lax.ppermute(partners, "expert", cores)
        return [
            (a, moved[c * count : (c + 1) * count]) for c, a in enumerate(mine)
        ]

    def added(*parts):
        return sum(a.astype(F32) for a in parts).astype(BF)

    rowwise = pl.BlockSpec((TILE, hidden), lambda i: (i, 0))
    grad_specs = [rowwise, rowwise, columns(hidden, TILE)]
    grad_types = [((half, hidden), BF), ((half, hidden), BF), ((hidden, half), BF)]

    def weight_grads(pair, old, *after):
        return call(
            functools.partial(grads_kernel, len(pair), bool(old)),
            list(zip(grad_types, grad_specs if old else [VMEM] * 3)),
            [
                (a, pl.BlockSpec(a.shape, lambda i: (0, 0)))
                for a in [items[k] for k in pair] + [d[k] for k in pair]
            ]
            + [(a, VMEM) for a in old],
            "grads_" + pair[0],
            after,
            vmem=24,
            grid=(half // TILE,),
        )

    load["oz"] = lax.ppermute(own, "expert", planes)
    load["sl"] = lax.ppermute(swapped, "pipe", peers)
    load["sz"] = lax.ppermute(load["sl"], "expert", planes)
    join("ol")
    t = gather(("ol",))
    (t,) = call(
        warm_kernel, [whole_out(16, LANES)], [(a, VMEM) for a in (gate, up, down)], "warm", (t,)
    )
    t = forward("ol", t)
    swap("ol", load["oz"], load["sl"])
    join("sl")
    join("oz", t)
    t = gather(("oz", "sl"), t)
    t = forward("oz", t, (theirs["sl"],))
    swap("oz")
    join("sz", t)
    t = gather(("sz",), t)
    t = forward("sl", t)
    t = forward("sz", t)
    swap("sz")
    t = backward(("sl", "sz"), t)
    swap("sl", t)
    half_grads = weight_grads(("sl", "sz"), [], t)
    sl, sz = combine(("sl", "sz"), (half_grads[0],))
    t = backward(("oz",), sl[0])
    extra_other = lax.ppermute(added(*sz), "expert", planes)
    (oz,) = combine(("oz",), t, (extra_other,))
    extra_own = lax.ppermute(added(*oz), "expert", planes)
    rest = lax.ppermute(added(*sl, extra_other), "pipe", peers)
    t = backward(("ol",), oz[0])
    grads = weight_grads(("oz", "ol"), half_grads, t)
    ((own_part, other_part),) = combine(("ol",), grads[0], (extra_own,), (rest,))
    (token_grad,) = call(
        finish_kernel,
        [whole_out(count, width)],
        [(block, SMEM), whole(own_part)]
        + [(a, VMEM) for a in (other_part, extra_own, rest)],
        "finish",
    )
    return (token_grad[None],) + tuple(g[None, None] for g in grads)


def solution(mesh):
    rank3 = P("pipe", "expert", None)
    rank4 = P("pipe", "expert", None, None)
    return jax.shard_map(
        local,
        mesh=mesh,
        in_specs=(rank3,) * 4 + (rank4,) * 3,
        out_specs=(rank3, rank4, rank4, rank4),
        check_vma=False,
    )
```

```python
import functools

import jax
import jax.numpy as jnp
from jax import lax
from jax.experimental import pallas as pl
from jax.experimental.pallas import tpu as pltpu
from jax.sharding import PartitionSpec as P

BF = jnp.bfloat16
F32 = jnp.float32
LANES = 128
TILE = 256
VMEM = pl.BlockSpec(memory_space=pltpu.VMEM)
SMEM = pl.BlockSpec(memory_space=pltpu.SMEM)
HBM = pl.BlockSpec(memory_space=pltpu.HBM)
ANY = pl.BlockSpec(memory_space=pl.ANY)


def call(kernel, outs, ins, name, after=(), scratch=(), copies=0, vmem=16, **more):
    ins = [a if isinstance(a, tuple) else (a, HBM) for a in ins]
    outs = [o if isinstance(o[1], pl.BlockSpec) else (o, HBM) for o in outs]
    count = len(ins)
    after = [a[0] if isinstance(a, tuple) else pinned(a) for a in after]

    def body(*refs):
        kernel(*refs[:count], *refs[count + len(after) :])

    return pl.pallas_call(
        body,
        out_shape=[
            (jax.ShapeDtypeStruct if spec is VMEM else pltpu.HBM)(*o) for o, spec in outs
        ],
        in_specs=[s for _, s in ins] + [ANY] * len(after),
        out_specs=[s for _, s in outs],
        scratch_shapes=list(scratch) + [pltpu.SemaphoreType.DMA((max(copies, 1),))],
        name=name,
        cost_estimate=pl.CostEstimate(
            flops=0, bytes_accessed=0, transcendentals=0
        ),
        compiler_params=pltpu.CompilerParams(vmem_limit_bytes=vmem * 2**20),
        **more,
    )(*[a if spec in (ANY, SMEM, VMEM) else pinned(a) for a, spec in ins], *after)


def pinned(a):
    if a.size * a.dtype.itemsize < 512:
        return a
    return pltpu.with_memory_space_constraint(a, pltpu.HBM)


def columns(rows, width, offset=0):
    return pl.BlockSpec((rows, width), lambda i: (0, i + offset))


class Copies:
    def __init__(self, sems):
        self.sems, self.made = sems, []

    def start(self, source, target):
        copy = pltpu.make_async_copy(source, target, self.sems.at[len(self.made)])
        copy.start()
        self.made.append(copy)
        return copy


def dot(a, b, contract):
    return lax.dot_general(
        a, b, ((contract[:1], contract[1:]), ((), ())), preferred_element_type=F32
    )


def pack_kernel(
    block_ref, tok_ref, grad_ref, ids_ref, probs_ref, own_ref, other_ref, sems
):
    half = tok_ref.shape[1] // 2
    first = block_ref[0] == 0
    for ref, at in ((tok_ref, 0), (grad_ref, half)):
        left, right = ref[:, :half], ref[:, half:]
        own_ref[:, at : at + half] = jnp.where(first, left, right)
        other_ref[:, at : at + half] = jnp.where(first, right, left)
    rest = probs_ref[...]
    parts = [ids_ref[...].astype(F32)]
    for _ in range(3):
        piece = rest.astype(BF).astype(F32)
        parts.append(piece)
        rest = rest - piece
    line = lax.broadcasted_iota(jnp.int32, (LANES, rest.shape[1]), 0)
    info = jnp.zeros(line.shape, F32)
    for n, part in enumerate(parts):
        for k in range(2):
            info = jnp.where(line == 2 * n + k, part[k : k + 1], info)
    info = info.T
    own_ref[:, 2 * half :] = info.astype(BF)
    other_ref[:, 2 * half :] = info.astype(BF)


def choose(members, info, chosen_ref, scale_ref):
    count = info.shape[1]
    capacity = chosen_ref.shape[0] // members.shape[0]
    match0 = members == info[0:1]
    match1 = members == info[1:2]
    prob0 = info[2:3] + info[4:5] + info[6:7]
    prob1 = info[3:4] + info[5:6] + info[7:8]
    routed = jnp.where(match0 | match1, 1.0, 0.0)
    coefficient = jnp.where(match0, prob0, 0.0) + jnp.where(match1, prob1, 0.0)
    earlier = lax.broadcasted_iota(jnp.int32, (count, count), 0)
    later = lax.broadcasted_iota(jnp.int32, (count, count), 1)
    before = jnp.where(earlier < later, 1.0, 0.0).astype(BF)
    slot = dot(routed.astype(BF), before, (1, 0))
    slot = jnp.where(routed > 0.5, slot, -1.0)
    ids = lax.broadcasted_iota(jnp.int32, (capacity, count), 0).astype(F32)
    for m in range(members.shape[0]):
        at = pl.ds(m * capacity, capacity)
        hit = ids == slot[m : m + 1]
        chosen_ref[at, :] = jnp.where(hit, 1.0, 0.0).astype(BF)
        scale_ref[at, :] = jnp.sum(
            jnp.where(hit, coefficient[m : m + 1], 0.0), axis=1, keepdims=True
        )


def gather_kernel(chunks, members_ref, *refs):
    n_loads, parts = 2 * chunks, 4
    load_refs, sent_refs = refs[:n_loads], refs[n_loads : n_loads + parts]
    chosen_refs = refs[n_loads + parts : 2 * n_loads + parts]
    loads, sent, chosens, scale, sems = refs[2 * n_loads + parts :]
    half = sent.shape[1] // 2
    capacity = sent.shape[0] // (n_loads * parts)
    copies = Copies(sems)
    first, second = slice(0, half), slice(half, 2 * half)
    info_at = slice(2 * half, 2 * half + LANES)
    ready = [
        [
            copies.start(ref.at[:, at], loads.at[n, :, at])
            for at in (info_at, first, second)
        ]
        for n, ref in enumerate(load_refs)
    ]
    out = []
    for n in range(n_loads):
        ready[n][0].wait()
        info = loads[n, :, info_at].astype(F32).T
        choose(members_ref[...], info, chosens.at[n], scale.at[n])
        out.append(copies.start(chosens.at[n], chosen_refs[n]))
    for m, at in enumerate((first, second)):
        for n in range(n_loads):
            ready[n][m + 1].wait()
            picked = dot(chosens[n], loads[n, :, at], (1, 0))
            if m:
                picked = picked * scale[n]
            picked = picked.astype(BF)
            for k in range(parts):
                row = (n_loads * k + n) * capacity
                sent[row : row + capacity, at] = picked[
                    k * capacity : (k + 1) * capacity
                ]
        for k in range(parts):
            rows = slice(n_loads * k * capacity, n_loads * (k + 1) * capacity)
            out.append(copies.start(sent.at[rows, at], sent_refs[k].at[:, at]))
    for copy in out:
        copy.wait()


def warm_kernel(gate_ref, up_ref, down_ref, out_ref, sems):
    out_ref[...] = jnp.zeros_like(out_ref)


def forward_kernel(offset, *refs):
    item_refs, (gate, up, down) = refs[:4], refs[4:7]
    sent_ref, whole_ref, items, sent, sems = refs[7:]
    half, hidden = gate.shape
    copies = Copies(sems)
    first, second = slice(0, half), slice(half, 2 * half)
    size = items.shape[0] // len(item_refs)
    held = slice(offset * size, (offset + 1) * size)

    def fetch(at):
        return [
            copies.start(ref.at[held, at], items.at[k * size : (k + 1) * size, at])
            for k, ref in enumerate(item_refs)
        ]

    x_in = fetch(first)
    dy_in = fetch(second)
    out = []
    for n, (ready, cols, w, contract) in enumerate(
        (
            (x_in, first, gate, (1, 0)),
            ([], first, up, (1, 0)),
            (dy_in, second, down, (1, 1)),
        )
    ):
        for copy in ready:
            copy.wait()
        at = slice(n * hidden, (n + 1) * hidden)
        sent[:, at] = dot(items[:, cols], w[...], contract).astype(BF)
        out.append(copies.start(sent.at[:, at], sent_ref.at[:, at]))
    out.append(copies.start(items, whole_ref))
    for copy in out:
        copy.wait()


def backward_kernel(chunks, *refs):
    mine_refs, theirs_refs = refs[:chunks], refs[chunks : 2 * chunks]
    gate, up = refs[2 * chunks : 2 * chunks + 2]
    d_refs = refs[2 * chunks + 2 : 3 * chunks + 2]
    contrib_refs = refs[3 * chunks + 2 : -5]
    mine, theirs, d, contrib, sems = refs[-5:]
    half, hidden = gate.shape
    rows = mine.shape[0] // chunks
    copies = Copies(sems)
    step = rows // 4
    size = rows // len(contrib_refs)
    parts = []
    for c in range(chunks):
        for r in range(0, rows, step):
            at, held = slice(r, r + step), slice(c * rows + r, c * rows + r + step)
            parts.append(
                (
                    copies.start(mine_refs[c].at[at], mine.at[held]),
                    copies.start(theirs_refs[c].at[at], theirs.at[held]),
                )
            )
    out = []
    for n, pair in enumerate(parts):
        at = slice(n * step, (n + 1) * step)
        for copy in pair:
            copy.wait()
        g, u, dh = [
            mine[at, m * hidden : (m + 1) * hidden].astype(F32)
            + theirs[at, m * hidden : (m + 1) * hidden].astype(F32)
            for m in range(3)
        ]
        sig = jax.nn.sigmoid(g)
        silu = g * sig
        d[at, :hidden] = (dh * u * sig * (1.0 + g * (1.0 - sig))).astype(BF)
        d[at, hidden : 2 * hidden] = (dh * silu).astype(BF)
        d[at, 2 * hidden :] = (silu * u).astype(BF)
        c, r = n // 4, n % 4 * step
        out.append(copies.start(d.at[at], d_refs[c].at[r : r + step]))
    for n in range(2):
        at = slice(n * half // 2, (n + 1) * half // 2)
        contrib[:, at] = (
            dot(d[:, :hidden], gate[at, :], (1, 1))
            + dot(d[:, hidden : 2 * hidden], up[at, :], (1, 1))
        ).astype(BF)
        for c in range(chunks):
            for k, ref in enumerate(contrib_refs):
                row = c * rows + k * size
                out.append(
                    copies.start(
                        contrib.at[row : row + size, at],
                        ref.at[c * size : (c + 1) * size, at],
                    )
                )
    for copy in out:
        copy.wait()


def combine_kernel(chunks, *refs):
    chosen_refs, got_refs = refs[: 2 * chunks], refs[2 * chunks : 2 * chunks + 4]
    out_refs, (got, sems) = refs[2 * chunks + 4 : -2], refs[-2:]
    copies = Copies(sems)
    capacity = got_refs[0].shape[0] // (2 * chunks)
    order = [(c, n) for n in (1, 0) for c in range(chunks)]
    ready = [
        [
            copies.start(
                ref.at[(2 * c + n) * capacity : (2 * c + n + 1) * capacity],
                got.at[2 * c + n, k * capacity : (k + 1) * capacity],
            )
            for k, ref in enumerate(got_refs)
        ]
        for c, n in order
    ]
    for (c, n), parts in zip(order, ready):
        for copy in parts:
            copy.wait()
        value = dot(chosen_refs[2 * c + n][...], got[2 * c + n], (0, 0)).astype(BF)
        out_refs[2 * c + n][...] = value


def finish_kernel(block_ref, a_ref, b_ref, c_ref, rest_ref, out_ref, sems):
    half = a_ref.shape[1]
    kept = sum(ref[...].astype(F32) for ref in (a_ref, b_ref, c_ref)).astype(BF)
    rest = rest_ref[...]
    first = block_ref[0] == 0
    out_ref[:, :half] = jnp.where(first, kept, rest)
    out_ref[:, half:] = jnp.where(first, rest, kept)


def grads_kernel(pairs, final, *refs):
    item_refs, d_refs = refs[:pairs], refs[pairs : 2 * pairs]
    old_refs, new_refs = refs[2 * pairs : -4], refs[-4:-1]
    hidden = new_refs[0].shape[1]
    half = item_refs[0].shape[1] // 2
    base = pl.multiple_of(pl.program_id(0) * TILE, TILE)
    tile = pl.ds(base, TILE)

    def write(n, value):
        at = (slice(None), tile) if n == 2 else (tile, slice(None))
        value = value.astype(BF)
        if final:
            value = (old_refs[n][at].astype(F32) + value.astype(F32)).astype(BF)
            new_refs[n][...] = value
        else:
            new_refs[n][at] = value

    for n in range(2):
        cols = slice(n * hidden, (n + 1) * hidden)
        write(
            n,
            sum(dot(x[:, tile], d[:, cols], (0, 0)) for x, d in zip(item_refs, d_refs)),
        )
    outer = sum(
        dot(y[:, pl.ds(base + half, TILE)], d[:, 2 * hidden :], (0, 0))
        for y, d in zip(item_refs, d_refs)
    )
    write(2, outer.T)


def local(tokens, grad_out, route_ids, route_probs, w_gate, w_up, w_down):
    pipes = lax.axis_size("pipe")
    experts = lax.axis_size("expert")
    block = lax.axis_index("pipe") // (pipes // 2)
    block = jnp.asarray(block, jnp.int32).reshape(1)
    plane = lax.axis_index("expert") // 2 % 2
    count, width = tokens.shape[1:]
    half, hidden = w_gate.shape[2:]
    capacity = 2 * count * route_ids.shape[2] // experts
    chips = experts // 4
    rows = experts * capacity // 2
    gate, up, down = w_gate[0, 0], w_up[0, 0], w_down[0, 0]

    peers = [(i, (i + pipes // 2) % pipes) for i in range(pipes)]
    planes = [(e, e ^ 2) for e in range(experts)]
    cores = [(e, e ^ 1) for e in range(experts)]
    turns = [[(e, (e + 4 * k) % experts) for e in range(experts)] for k in range(chips)]
    backs = [[(f, e) for e, f in turn] for turn in turns]
    here = lax.axis_index("expert")
    members = (here + 4 * jnp.arange(chips, dtype=jnp.int32)) % experts
    members = members.astype(F32)[:, None]

    def spread(parts, routes):
        moved = [lax.ppermute(a, "expert", r) for a, r in zip(parts[1:], routes[1:])]
        return [parts[0]] + moved

    def whole(a):
        return a, pl.BlockSpec(a.shape)

    def whole_out(*shape):
        return (shape, BF), pl.BlockSpec(shape)

    packed = whole_out(count, width + LANES)
    own, swapped = call(
        pack_kernel,
        [packed, packed],
        [(block, SMEM)]
        + [
            whole(a)
            for a in (tokens[0], grad_out[0], route_ids[0].T, route_probs[0].T)
        ],
        "pack",
    )
    load = {"ol": own}
    partner = {"ol": "sl", "sl": "ol", "oz": "sz", "sz": "oz"}
    chosen, pieces, items, theirs, d, got, outgoing, other = ({} for _ in range(8))

    weights = [(a, VMEM) for a in (gate, up, down)]

    def buffers(*shapes):
        return [pltpu.VMEM(s, BF) for s in shapes]

    def gather(keys, *after):
        n = len(keys)
        loads = [
            a if a is own else (a, ANY) for k in keys for a in (load[k], other[k])
        ]
        out = call(
            functools.partial(gather_kernel, n),
            [((2 * n * capacity, width), BF)] * chips
            + [((rows // 2, count), BF)] * (2 * n),
            [whole(members)] + loads,
            "gather_" + "_".join(keys),
            after,
            buffers(
                (2 * n, count, width + LANES),
                (n * rows, width),
                (2 * n, rows // 2, count),
            )
            + [pltpu.VMEM((2 * n, rows // 2, 1), F32)],
            8 * n + 8,
        )
        moved = spread(out[:chips], turns)
        for c, k in enumerate(keys):
            chosen[k] = out[chips + 2 * c : chips + 2 * c + 2]
            pieces[k] = c, moved
        return out[0]

    def forward(k, *after):
        offset, moved = pieces[k]
        outgoing[k], items[k] = call(
            functools.partial(forward_kernel, offset),
            [((rows, 3 * hidden), BF), ((rows, width), BF)],
            [moved[0]] + [(a, ANY) for a in moved[1:]] + weights,
            "forward_" + k,
            after,
            buffers((rows, width), (rows, 3 * hidden)),
            16,
        )
        return outgoing[k]

    def swap(k, *after):
        out, *_ = lax.optimization_barrier((outgoing[k], *after))
        theirs[partner[k]] = lax.ppermute(out, "pipe", peers)

    def join(k, *after):
        mine, *_ = lax.optimization_barrier((load[k], *after))
        other[k] = lax.ppermute(mine, "expert", cores)

    def backward(keys, *after):
        n = len(keys)
        out = call(
            functools.partial(backward_kernel, n),
            [((rows, 3 * hidden), BF)] * n + [((2 * n * capacity, half), BF)] * chips,
            [outgoing[k] for k in keys]
            + [(theirs[k], ANY) for k in keys]
            + weights[:2],
            "backward_" + "_".join(keys),
            after,
            buffers(
                (n * rows, 3 * hidden),
                (n * rows, 3 * hidden),
                (n * rows, 3 * hidden),
                (n * rows, half),
            ),
            20 * n + 2,
            vmem=24,
        )
        d.update(zip(keys, out))
        got[keys] = spread(out[n:], backs)
        return out[0]

    def combine(keys, *after):
        n = len(keys)
        out = call(
            functools.partial(combine_kernel, n),
            [(((count, half), BF), VMEM)] * (2 * n),
            [whole(a) for k in keys for a in chosen[k]]
            + [got[keys][0]]
            + [(a, ANY) for a in got[keys][1:]],
            "combine_" + "_".join(keys),
            after,
            buffers((2 * n, rows // 2, half)),
            8 * n,
        )
        return [
            (out[c], lax.ppermute(out[c + 1], "expert", cores))
            for c in range(0, 2 * n, 2)
        ]

    def added(*parts):
        return sum(a.astype(F32) for a in parts).astype(BF)

    rowwise = pl.BlockSpec((TILE, hidden), lambda i: (i, 0))
    grad_specs = [rowwise, rowwise, columns(hidden, TILE)]
    grad_types = [((half, hidden), BF), ((half, hidden), BF), ((hidden, half), BF)]

    def weight_grads(pair, old, *after):
        return call(
            functools.partial(grads_kernel, len(pair), bool(old)),
            list(zip(grad_types, grad_specs if old else [VMEM] * 3)),
            [
                (a, pl.BlockSpec(a.shape, lambda i: (0, 0)))
                for a in [items[k] for k in pair] + [d[k] for k in pair]
            ]
            + [(a, VMEM) for a in old],
            "grads_" + pair[0],
            after,
            vmem=24,
            grid=(half // TILE,),
        )

    load["oz"] = lax.ppermute(own, "expert", planes)
    load["sl"] = lax.ppermute(swapped, "pipe", peers)
    load["sz"] = lax.ppermute(load["sl"], "expert", planes)
    join("ol")
    t = gather(("ol",))
    (t,) = call(
        warm_kernel, [whole_out(16, LANES)], [(a, VMEM) for a in (gate, up, down)], "warm", (t,)
    )
    t = forward("ol", t)
    swap("ol", load["oz"], load["sl"])
    join("oz", t)
    t = gather(("oz",), t)
    join("sl")
    t = gather(("sl",), t)
    t = forward("oz", t, (theirs["sl"],), (load["sz"],))
    swap("oz")
    join("sz", t)
    t = gather(("sz",), t)
    t = forward("sl", t)
    t = forward("sz", t)
    swap("sz")
    t = backward(("sl", "sz"), t)
    swap("sl", t)
    half_grads = weight_grads(("sl", "sz"), [], t)
    sl, sz = combine(("sl", "sz"), (half_grads[0],))
    t = backward(("oz",), (sl[0],))
    extra_other = lax.ppermute(added(*sz), "expert", planes)
    (oz,) = combine(("oz",), t)
    extra_own = lax.ppermute(added(*oz), "expert", planes)
    rest = lax.ppermute(added(*sl, extra_other), "pipe", peers)
    t = backward(("ol",), (oz[0],), (extra_other,))
    grads = weight_grads(("oz", "ol"), half_grads, t)
    ((own_part, other_part),) = combine(("ol",), grads[0], (extra_own,), (rest,))
    (token_grad,) = call(
        finish_kernel,
        [whole_out(count, width)],
        [(block, SMEM)]
        + [(a, VMEM) for a in (own_part, other_part, extra_own, rest)],
        "finish",
    )
    return (token_grad[None],) + tuple(g[None, None] for g in grads)


def solution(mesh):
    rank3 = P("pipe", "expert", None)
    rank4 = P("pipe", "expert", None, None)
    return jax.shard_map(
        local,
        mesh=mesh,
        in_specs=(rank3,) * 4 + (rank4,) * 3,
        out_specs=(rank3, rank4, rank4, rank4),
        check_vma=False,
    )
```

```python
import functools

import jax
import jax.numpy as jnp
from jax import lax
from jax.experimental import pallas as pl
from jax.experimental.pallas import tpu as pltpu
from jax.sharding import PartitionSpec as P

BF = jnp.bfloat16
F32 = jnp.float32
LANES = 128
TILE = 256
VMEM = pl.BlockSpec(memory_space=pltpu.VMEM)
SMEM = pl.BlockSpec(memory_space=pltpu.SMEM)
HBM = pl.BlockSpec(memory_space=pltpu.HBM)
ANY = pl.BlockSpec(memory_space=pl.ANY)


def call(kernel, outs, ins, name, after=(), scratch=(), copies=0, vmem=16, **more):
    ins = [a if isinstance(a, tuple) else (a, HBM) for a in ins]
    outs = [o if isinstance(o[1], pl.BlockSpec) else (o, HBM) for o in outs]
    count = len(ins)
    after = [a[0] if isinstance(a, tuple) else pinned(a) for a in after]

    def body(*refs):
        kernel(*refs[:count], *refs[count + len(after) :])

    return pl.pallas_call(
        body,
        out_shape=[
            (jax.ShapeDtypeStruct if spec is VMEM else pltpu.HBM)(*o) for o, spec in outs
        ],
        in_specs=[s for _, s in ins] + [ANY] * len(after),
        out_specs=[s for _, s in outs],
        scratch_shapes=list(scratch) + [pltpu.SemaphoreType.DMA((max(copies, 1),))],
        name=name,
        cost_estimate=pl.CostEstimate(
            flops=0, bytes_accessed=0, transcendentals=0
        ),
        compiler_params=pltpu.CompilerParams(vmem_limit_bytes=vmem * 2**20),
        **more,
    )(*[a if spec in (ANY, SMEM, VMEM) else pinned(a) for a, spec in ins], *after)


def pinned(a):
    if a.size * a.dtype.itemsize < 512:
        return a
    return pltpu.with_memory_space_constraint(a, pltpu.HBM)


def columns(rows, width, offset=0):
    return pl.BlockSpec((rows, width), lambda i: (0, i + offset))


class Copies:
    def __init__(self, sems):
        self.sems, self.made = sems, []

    def start(self, source, target):
        copy = pltpu.make_async_copy(source, target, self.sems.at[len(self.made)])
        copy.start()
        self.made.append(copy)
        return copy


def dot(a, b, contract):
    return lax.dot_general(
        a, b, ((contract[:1], contract[1:]), ((), ())), preferred_element_type=F32
    )


def pack_kernel(
    block_ref, tok_ref, grad_ref, ids_ref, probs_ref, own_ref, other_ref, sems
):
    half = tok_ref.shape[1] // 2
    first = block_ref[0] == 0
    for ref, at in ((tok_ref, 0), (grad_ref, half)):
        left, right = ref[:, :half], ref[:, half:]
        own_ref[:, at : at + half] = jnp.where(first, left, right)
        other_ref[:, at : at + half] = jnp.where(first, right, left)
    rest = probs_ref[...]
    parts = [ids_ref[...].astype(F32)]
    for _ in range(3):
        piece = rest.astype(BF).astype(F32)
        parts.append(piece)
        rest = rest - piece
    line = lax.broadcasted_iota(jnp.int32, (LANES, rest.shape[1]), 0)
    info = jnp.zeros(line.shape, F32)
    for n, part in enumerate(parts):
        for k in range(2):
            info = jnp.where(line == 2 * n + k, part[k : k + 1], info)
    info = info.T
    own_ref[:, 2 * half :] = info.astype(BF)
    other_ref[:, 2 * half :] = info.astype(BF)


def choose(members, info, chosen_ref, scale_ref):
    count = info.shape[1]
    capacity = chosen_ref.shape[0] // members.shape[0]
    match0 = members == info[0:1]
    match1 = members == info[1:2]
    prob0 = info[2:3] + info[4:5] + info[6:7]
    prob1 = info[3:4] + info[5:6] + info[7:8]
    routed = jnp.where(match0 | match1, 1.0, 0.0)
    coefficient = jnp.where(match0, prob0, 0.0) + jnp.where(match1, prob1, 0.0)
    earlier = lax.broadcasted_iota(jnp.int32, (count, count), 0)
    later = lax.broadcasted_iota(jnp.int32, (count, count), 1)
    before = jnp.where(earlier < later, 1.0, 0.0).astype(BF)
    slot = dot(routed.astype(BF), before, (1, 0))
    slot = jnp.where(routed > 0.5, slot, -1.0)
    ids = lax.broadcasted_iota(jnp.int32, (capacity, count), 0).astype(F32)
    for m in range(members.shape[0]):
        at = pl.ds(m * capacity, capacity)
        hit = ids == slot[m : m + 1]
        chosen_ref[at, :] = jnp.where(hit, 1.0, 0.0).astype(BF)
        scale_ref[at, :] = jnp.sum(
            jnp.where(hit, coefficient[m : m + 1], 0.0), axis=1, keepdims=True
        )


def gather_kernel(chunks, members_ref, *refs):
    n_loads, parts = 2 * chunks, 4
    load_refs, sent_refs = refs[:n_loads], refs[n_loads : n_loads + parts]
    chosen_refs = refs[n_loads + parts : 2 * n_loads + parts]
    loads, sent, chosens, scale, sems = refs[2 * n_loads + parts :]
    half = sent.shape[1] // 2
    capacity = sent.shape[0] // (n_loads * parts)
    copies = Copies(sems)
    first, second = slice(0, half), slice(half, 2 * half)
    info_at = slice(2 * half, 2 * half + LANES)
    ready = [
        [
            copies.start(ref.at[:, at], loads.at[n, :, at])
            for at in (info_at, first, second)
        ]
        for n, ref in enumerate(load_refs)
    ]
    out = []
    for n in range(n_loads):
        ready[n][0].wait()
        info = loads[n, :, info_at].astype(F32).T
        choose(members_ref[...], info, chosens.at[n], scale.at[n])
        out.append(copies.start(chosens.at[n], chosen_refs[n]))
    for m, at in enumerate((first, second)):
        for n in range(n_loads):
            ready[n][m + 1].wait()
            picked = dot(chosens[n], loads[n, :, at], (1, 0))
            if m:
                picked = picked * scale[n]
            picked = picked.astype(BF)
            for k in range(parts):
                row = (n_loads * k + n) * capacity
                sent[row : row + capacity, at] = picked[
                    k * capacity : (k + 1) * capacity
                ]
        for k in range(parts):
            rows = slice(n_loads * k * capacity, n_loads * (k + 1) * capacity)
            out.append(copies.start(sent.at[rows, at], sent_refs[k].at[:, at]))
    for copy in out:
        copy.wait()


def warm_kernel(gate_ref, up_ref, down_ref, out_ref, sems):
    out_ref[...] = jnp.zeros_like(out_ref)


def forward_kernel(offset, *refs):
    item_refs, (gate, up, down) = refs[:4], refs[4:7]
    sent_ref, whole_ref, items, sent, sems = refs[7:]
    half, hidden = gate.shape
    copies = Copies(sems)
    first, second = slice(0, half), slice(half, 2 * half)
    size = items.shape[0] // len(item_refs)
    held = slice(offset * size, (offset + 1) * size)

    def fetch(at):
        return [
            copies.start(ref.at[held, at], items.at[k * size : (k + 1) * size, at])
            for k, ref in enumerate(item_refs)
        ]

    x_in = fetch(first)
    dy_in = fetch(second)
    out = []
    for n, (ready, cols, w, contract) in enumerate(
        (
            (x_in, first, gate, (1, 0)),
            ([], first, up, (1, 0)),
            (dy_in, second, down, (1, 1)),
        )
    ):
        for copy in ready:
            copy.wait()
        at = slice(n * hidden, (n + 1) * hidden)
        sent[:, at] = dot(items[:, cols], w[...], contract).astype(BF)
        out.append(copies.start(sent.at[:, at], sent_ref.at[:, at]))
    out.append(copies.start(items, whole_ref))
    for copy in out:
        copy.wait()


def backward_kernel(chunks, *refs):
    mine_refs, theirs_refs = refs[:chunks], refs[chunks : 2 * chunks]
    gate, up = refs[2 * chunks : 2 * chunks + 2]
    d_refs = refs[2 * chunks + 2 : 3 * chunks + 2]
    contrib_refs = refs[3 * chunks + 2 : -5]
    mine, theirs, d, contrib, sems = refs[-5:]
    half, hidden = gate.shape
    rows = mine.shape[0] // chunks
    copies = Copies(sems)
    step = rows // 4
    size = rows // len(contrib_refs)
    parts = []
    for c in range(chunks):
        for r in range(0, rows, step):
            at, held = slice(r, r + step), slice(c * rows + r, c * rows + r + step)
            parts.append(
                (
                    copies.start(mine_refs[c].at[at], mine.at[held]),
                    copies.start(theirs_refs[c].at[at], theirs.at[held]),
                )
            )
    out = []
    for n, pair in enumerate(parts):
        at = slice(n * step, (n + 1) * step)
        for copy in pair:
            copy.wait()
        g, u, dh = [
            mine[at, m * hidden : (m + 1) * hidden].astype(F32)
            + theirs[at, m * hidden : (m + 1) * hidden].astype(F32)
            for m in range(3)
        ]
        sig = jax.nn.sigmoid(g)
        silu = g * sig
        d[at, :hidden] = (dh * u * sig * (1.0 + g * (1.0 - sig))).astype(BF)
        d[at, hidden : 2 * hidden] = (dh * silu).astype(BF)
        d[at, 2 * hidden :] = (silu * u).astype(BF)
        c, r = n // 4, n % 4 * step
        out.append(copies.start(d.at[at], d_refs[c].at[r : r + step]))
    for n in range(2):
        at = slice(n * half // 2, (n + 1) * half // 2)
        contrib[:, at] = (
            dot(d[:, :hidden], gate[at, :], (1, 1))
            + dot(d[:, hidden : 2 * hidden], up[at, :], (1, 1))
        ).astype(BF)
        for c in range(chunks):
            for k, ref in enumerate(contrib_refs):
                row = c * rows + k * size
                out.append(
                    copies.start(
                        contrib.at[row : row + size, at],
                        ref.at[c * size : (c + 1) * size, at],
                    )
                )
    for copy in out:
        copy.wait()


def combine_kernel(chunks, *refs):
    chosen_refs, got_refs = refs[: 2 * chunks], refs[2 * chunks : 2 * chunks + 4]
    out_refs, (got, sems) = refs[2 * chunks + 4 : -2], refs[-2:]
    copies = Copies(sems)
    capacity = got_refs[0].shape[0] // (2 * chunks)
    order = [(c, n) for n in (1, 0) for c in range(chunks)]
    ready = [
        [
            copies.start(
                ref.at[(2 * c + n) * capacity : (2 * c + n + 1) * capacity],
                got.at[2 * c + n, k * capacity : (k + 1) * capacity],
            )
            for k, ref in enumerate(got_refs)
        ]
        for c, n in order
    ]
    for (c, n), parts in zip(order, ready):
        for copy in parts:
            copy.wait()
        value = dot(chosen_refs[2 * c + n][...], got[2 * c + n], (0, 0)).astype(BF)
        out_refs[2 * c + n][...] = value


def finish_kernel(block_ref, a_ref, b_ref, c_ref, rest_ref, out_ref, sems):
    half = a_ref.shape[1]
    kept = sum(ref[...].astype(F32) for ref in (a_ref, b_ref, c_ref)).astype(BF)
    rest = rest_ref[...]
    first = block_ref[0] == 0
    out_ref[:, :half] = jnp.where(first, kept, rest)
    out_ref[:, half:] = jnp.where(first, rest, kept)


def grads_kernel(pairs, final, *refs):
    item_refs, d_refs = refs[:pairs], refs[pairs : 2 * pairs]
    old_refs, new_refs = refs[2 * pairs : -4], refs[-4:-1]
    hidden = new_refs[0].shape[1]
    half = item_refs[0].shape[1] // 2
    base = pl.multiple_of(pl.program_id(0) * TILE, TILE)
    tile = pl.ds(base, TILE)

    def write(n, value):
        at = (slice(None), tile) if n == 2 else (tile, slice(None))
        value = value.astype(BF)
        if final:
            value = (old_refs[n][at].astype(F32) + value.astype(F32)).astype(BF)
            new_refs[n][...] = value
        else:
            new_refs[n][at] = value

    for n in range(2):
        cols = slice(n * hidden, (n + 1) * hidden)
        write(
            n,
            sum(dot(x[:, tile], d[:, cols], (0, 0)) for x, d in zip(item_refs, d_refs)),
        )
    outer = sum(
        dot(y[:, pl.ds(base + half, TILE)], d[:, 2 * hidden :], (0, 0))
        for y, d in zip(item_refs, d_refs)
    )
    write(2, outer.T)


def local(tokens, grad_out, route_ids, route_probs, w_gate, w_up, w_down):
    pipes = lax.axis_size("pipe")
    experts = lax.axis_size("expert")
    block = lax.axis_index("pipe") // (pipes // 2)
    block = jnp.asarray(block, jnp.int32).reshape(1)
    plane = lax.axis_index("expert") // 2 % 2
    count, width = tokens.shape[1:]
    half, hidden = w_gate.shape[2:]
    capacity = 2 * count * route_ids.shape[2] // experts
    chips = experts // 4
    rows = experts * capacity // 2
    gate, up, down = w_gate[0, 0], w_up[0, 0], w_down[0, 0]

    peers = [(i, (i + pipes // 2) % pipes) for i in range(pipes)]
    planes = [(e, e ^ 2) for e in range(experts)]
    cores = [(e, e ^ 1) for e in range(experts)]
    turns = [[(e, (e + 4 * k) % experts) for e in range(experts)] for k in range(chips)]
    backs = [[(f, e) for e, f in turn] for turn in turns]
    here = lax.axis_index("expert")
    members = (here + 4 * jnp.arange(chips, dtype=jnp.int32)) % experts
    members = members.astype(F32)[:, None]

    def spread(parts, routes):
        moved = [lax.ppermute(a, "expert", r) for a, r in zip(parts[1:], routes[1:])]
        return [parts[0]] + moved

    def whole(a):
        return a, pl.BlockSpec(a.shape)

    def whole_out(*shape):
        return (shape, BF), pl.BlockSpec(shape)

    packed = whole_out(count, width + LANES)
    own, swapped = call(
        pack_kernel,
        [packed, packed],
        [(block, SMEM)]
        + [
            whole(a)
            for a in (tokens[0], grad_out[0], route_ids[0].T, route_probs[0].T)
        ],
        "pack",
    )
    load = {"ol": own}
    partner = {"ol": "sl", "sl": "ol", "oz": "sz", "sz": "oz"}
    chosen, pieces, items, theirs, d, got, outgoing, other = ({} for _ in range(8))

    weights = [(a, VMEM) for a in (gate, up, down)]

    def buffers(*shapes):
        return [pltpu.VMEM(s, BF) for s in shapes]

    def gather(keys, *after):
        n = len(keys)
        loads = [
            a if a is own else (a, ANY) for k in keys for a in (load[k], other[k])
        ]
        out = call(
            functools.partial(gather_kernel, n),
            [((2 * n * capacity, width), BF)] * chips
            + [((rows // 2, count), BF)] * (2 * n),
            [whole(members)] + loads,
            "gather_" + "_".join(keys),
            after,
            buffers(
                (2 * n, count, width + LANES),
                (n * rows, width),
                (2 * n, rows // 2, count),
            )
            + [pltpu.VMEM((2 * n, rows // 2, 1), F32)],
            8 * n + 8,
        )
        moved = spread(out[:chips], turns)
        for c, k in enumerate(keys):
            chosen[k] = out[chips + 2 * c : chips + 2 * c + 2]
            pieces[k] = c, moved
        return out[0]

    def forward(k, *after):
        offset, moved = pieces[k]
        outgoing[k], items[k] = call(
            functools.partial(forward_kernel, offset),
            [((rows, 3 * hidden), BF), ((rows, width), BF)],
            [moved[0]] + [(a, ANY) for a in moved[1:]] + weights,
            "forward_" + k,
            after,
            buffers((rows, width), (rows, 3 * hidden)),
            16,
        )
        return outgoing[k]

    def swap(k, *after):
        out, *_ = lax.optimization_barrier((outgoing[k], *after))
        theirs[partner[k]] = lax.ppermute(out, "pipe", peers)

    def join(k, *after):
        mine, *_ = lax.optimization_barrier((load[k], *after))
        other[k] = lax.ppermute(mine, "expert", cores)

    def backward(keys, *after):
        n = len(keys)
        out = call(
            functools.partial(backward_kernel, n),
            [((rows, 3 * hidden), BF)] * n + [((2 * n * capacity, half), BF)] * chips,
            [outgoing[k] for k in keys]
            + [(theirs[k], ANY) for k in keys]
            + weights[:2],
            "backward_" + "_".join(keys),
            after,
            buffers(
                (n * rows, 3 * hidden),
                (n * rows, 3 * hidden),
                (n * rows, 3 * hidden),
                (n * rows, half),
            ),
            20 * n + 2,
            vmem=24,
        )
        d.update(zip(keys, out))
        got[keys] = spread(out[n:], backs)
        return out[0]

    def combine(keys, *after):
        n = len(keys)
        out = call(
            functools.partial(combine_kernel, n),
            [(((count, half), BF), VMEM)] * (2 * n),
            [whole(a) for k in keys for a in chosen[k]]
            + [got[keys][0]]
            + [(a, ANY) for a in got[keys][1:]],
            "combine_" + "_".join(keys),
            after,
            buffers((2 * n, rows // 2, half)),
            8 * n,
        )
        return [
            (out[c], lax.ppermute(out[c + 1], "expert", cores))
            for c in range(0, 2 * n, 2)
        ]

    def added(*parts):
        return sum(a.astype(F32) for a in parts).astype(BF)

    rowwise = pl.BlockSpec((TILE, hidden), lambda i: (i, 0))
    grad_specs = [rowwise, rowwise, columns(hidden, TILE)]
    grad_types = [((half, hidden), BF), ((half, hidden), BF), ((hidden, half), BF)]

    def weight_grads(pair, old, *after):
        return call(
            functools.partial(grads_kernel, len(pair), bool(old)),
            list(zip(grad_types, grad_specs if old else [VMEM] * 3)),
            [
                (a, pl.BlockSpec(a.shape, lambda i: (0, 0)))
                for a in [items[k] for k in pair] + [d[k] for k in pair]
            ]
            + [(a, VMEM) for a in old],
            "grads_" + pair[0],
            after,
            vmem=24,
            grid=(half // TILE,),
        )

    load["oz"] = lax.ppermute(own, "expert", planes)
    load["sl"] = lax.ppermute(swapped, "pipe", peers)
    load["sz"] = lax.ppermute(load["sl"], "expert", planes)
    join("ol")
    t = gather(("ol",))
    (t,) = call(
        warm_kernel, [whole_out(16, LANES)], [(a, VMEM) for a in (gate, up, down)], "warm", (t,)
    )
    t = forward("ol", t)
    swap("ol", load["oz"], load["sl"])
    join("oz", t)
    t = gather(("oz",), t)
    join("sl")
    t = gather(("sl",), t)
    t = forward("oz", t)
    swap("oz", load["sz"], theirs["sl"])
    join("sz", t)
    t = gather(("sz",), t)
    t = forward("sl", t)
    t = forward("sz", t)
    swap("sz")
    t = backward(("sl", "sz"), t)
    swap("sl", t)
    half_grads = weight_grads(("sl", "sz"), [], t)
    sl, sz = combine(("sl", "sz"), (half_grads[0],))
    t = backward(("oz",), (sl[0],))
    extra_other = lax.ppermute(added(*sz), "expert", planes)
    (oz,) = combine(("oz",), t)
    extra_own = lax.ppermute(added(*oz), "expert", planes)
    rest = lax.ppermute(added(*sl, extra_other), "pipe", peers)
    t = backward(("ol",), (oz[0],), (extra_other,))
    grads = weight_grads(("oz", "ol"), half_grads, t)
    ((own_part, other_part),) = combine(("ol",), grads[0], (extra_own,), (rest,))
    (token_grad,) = call(
        finish_kernel,
        [whole_out(count, width)],
        [(block, SMEM)]
        + [(a, VMEM) for a in (own_part, other_part, extra_own, rest)],
        "finish",
    )
    return (token_grad[None],) + tuple(g[None, None] for g in grads)


def solution(mesh):
    rank3 = P("pipe", "expert", None)
    rank4 = P("pipe", "expert", None, None)
    return jax.shard_map(
        local,
        mesh=mesh,
        in_specs=(rank3,) * 4 + (rank4,) * 3,
        out_specs=(rank3, rank4, rank4, rank4),
        check_vma=False,
    )
```
